32 devices in a mesh: tm: 2 (over y), blk: 16 (over z, x, core).
Axes of the slice: x: 2, y: 2, z: 4, core: 2. Of those that a mesh axis runs over, the one named last changes fastest.
Arguments:
- propagator: float32 [2, 8192, 2048], P('tm', 'blk'), may hold values from -0.09375 to 0.09375
- inv_diag: float32 [2, 8192, 2048], P('tm', 'blk'), may hold values from -0.09375 to 0.09375
- rhs: float32 [2, 4096, 128], P('tm', 'blk'), may hold values from -6 to 6
- arrow: float32 [2, 64, 4096], P('tm', None, 'blk'), may hold values from -0.0625 to 0.0625
- tip_inv: float32 [64, 64], replicated, may hold values from -0.75 to 0.75
- tip_rhs: float32 [64, 128], replicated, may hold values from -6 to 6
Outputs:
- solved: float32 [2, 4096, 128], P('tm', 'blk')
- tip: float32 [64, 128], replicated
The draws below stay inside these ranges and needn't reach their ends.
All inputs are finite; a program needn't handle non-finite values.
Results may differ from the reference program's by a relative error of at most 0.00011.
Values sent between devices are 32-bit elements; how exact they have to be, the bound alone decides.
No kernel may reach another device: no remote copies, remote signals or barrier semaphores. Data moves between devices by JAX's collectives and lax.ppermute only.
A program may use at most 64 MiB of HBM per device.

```python
import jax
import jax.numpy as jnp
from jax import lax

NS = 4096
NF = 64
RHS = 128
GROUP = 8
NT = 2
PIECE = 256
TILE_ROWS = 512
TILE_COLS = 2048
N_BLK = 16


def levels(own_key, dims, shards, least, top_value):
    loudness = 1.0
    for axis_at, shards_of in shards:
        heights = jax.random.uniform(jax.random.fold_in(jax.random.fold_in(own_key, 6), axis_at), (shards_of,), jnp.float32, least / len(shards), top_value / len(shards))
        loudness = loudness * jnp.repeat(jnp.exp(heights), dims[axis_at] // shards_of).reshape((-1,) + (1,) * (len(dims) - 1 - axis_at))
    return loudness


def scatter_about(stream_key, dims, width, reach, split=(), kind=jnp.bfloat16):
    gain = levels(stream_key, dims, split, -0.22, 0.18) if split else 1.0
    drawn = jax.random.normal(stream_key, dims, jnp.float32) * width * gain
    return jnp.minimum(jnp.maximum(drawn, -reach), reach).astype(kind)


def setup_inputs(seed: int = 0) -> dict:
    keys = jax.random.split(jax.random.key(seed), 7)
    propagator = scatter_about(keys[0], (NT, N_BLK * TILE_ROWS, TILE_COLS), NS ** -0.5, 0.09375, ((0, 2), (1, 16)), jnp.float32)
    inv_diag = scatter_about(keys[1], (NT, N_BLK * TILE_ROWS, TILE_COLS), NS ** -0.5, 0.09375, ((0, 2), (1, 16)), jnp.float32)
    rhs = scatter_about(keys[2], (NT, NS, RHS), 1.0, 6.0, ((0, 2), (1, 16)), jnp.float32)
    arrow = scatter_about(keys[3], (NT, NF, NS), (NS * NT) ** -0.5, 0.0625, ((0, 2), (2, 16)), jnp.float32)
    tip_inv = scatter_about(keys[4], (NF, NF), NF ** -0.5, 0.75, (), jnp.float32)
    tip_rhs = scatter_about(keys[5], (NF, RHS), 1.0, 6.0, (), jnp.float32)
    return dict(propagator=propagator, inv_diag=inv_diag, rhs=rhs, arrow=arrow, tip_inv=tip_inv, tip_rhs=tip_rhs)


HIGHEST_PREC = lax.Precision.HIGHEST


def assemble_full(tiles):
    high_count = N_BLK // GROUP
    shaped = tiles.reshape(high_count, GROUP, high_count, PIECE, TILE_COLS)
    return jnp.transpose(shaped, (2, 1, 3, 0, 4)).reshape(NS, NS)


def reference(propagator, inv_diag, rhs, arrow, tip_inv, tip_rhs):
    def advance(earlier, slices):
        tiles_m, tiles_g, right_side, arrow_rows = slices
        matrix_m = assemble_full(tiles_m)
        matrix_g = assemble_full(tiles_g)
        local_term = jnp.dot(matrix_g, right_side, precision=HIGHEST_PREC, preferred_element_type=jnp.float32)
        current = local_term - jnp.dot(matrix_m, earlier, precision=HIGHEST_PREC, preferred_element_type=jnp.float32)
        partial_tip = jnp.dot(arrow_rows, current, precision=HIGHEST_PREC, preferred_element_type=jnp.float32)
        return current, (current, partial_tip)

    starting = jnp.zeros((NS, RHS), jnp.float32)
    _, (solved, partials) = lax.scan(advance, starting, (propagator, inv_diag, rhs, arrow))
    reduced = tip_rhs - jnp.sum(partials, axis=0)
    tip = jnp.dot(tip_inv, reduced, precision=HIGHEST_PREC, preferred_element_type=jnp.float32)
    return solved, tip
```

```python
import jax
import jax.numpy as jnp
from jax import lax
from jax.sharding import PartitionSpec as P

GROUP = 8
AXES = ("tm", "blk")
HIGH = lax.Precision.HIGH


def dot(a, b):
    return jnp.dot(a, b, precision=HIGH, preferred_element_type=jnp.float32)


def on_device(propagator, inv_diag, rhs, arrow, tip_inv, tip_rhs):
    steps = lax.axis_size("tm")
    blocks = lax.axis_size("blk")
    high_count = blocks // GROUP
    position = lax.axis_index("blk")
    low = position % GROUP
    high = position // GROUP
    piece = rhs.shape[1]
    width = rhs.shape[2]

    def move(value, flip, sources=None, ahead=0):
        sources = range(steps) if sources is None else sources
        route = [
            (t * blocks + b, (t + ahead) * blocks + (b ^ flip))
            for t in sources
            for b in range(blocks)
        ]
        return lax.ppermute(value, AXES, route)

    def gather(own, sources=None):
        parts = {0: own}
        for flip in range(2, GROUP, 2):
            parts[flip] = move(own, flip, sources)
        for flip in range(0, GROUP, 2):
            parts[flip + 1] = move(parts[flip], 1, sources)
        return parts

    def apply_tile(tile, parts):
        columns = jnp.zeros((tile.shape[1], width), jnp.float32)
        for flip, part in parts.items():
            columns = lax.dynamic_update_slice_in_dim(columns, part, (low ^ flip) * piece, 0)
        return dot(tile, columns)

    def row_block(partial, flip):
        return lax.dynamic_slice_in_dim(partial, (high ^ flip) * piece, piece, 0)

    partial = apply_tile(inv_diag[0], gather(rhs[0]))
    for t in range(steps - 1):
        earlier = sum(
            move(row_block(partial, e), e * GROUP, (t,), 1) for e in range(high_count)
        )
        partial = partial - apply_tile(propagator[0], gather(earlier, (t + 1,)))

    solved = row_block(partial, 0)
    for e in range(1, high_count):
        solved = solved + move(row_block(partial, e), e * GROUP)

    arrows = [arrow[0]] + [move(arrow[0], e * GROUP) for e in range(1, high_count)]
    terms = sum(dot(arrows[e], row_block(partial, e)) for e in range(high_count))
    flips = [1 << k for k in range(blocks.bit_length() - 1)]
    terms = terms + move(terms, flips[0])
    terms = terms + move(terms, flips[1]) + move(terms, flips[2]) + move(terms, flips[1] | flips[2])
    for flip in flips[3:]:
        terms = terms + move(terms, flip)
    for k in range(steps.bit_length() - 1):
        ring = [
            (t * blocks + b, (t ^ 1 << k) * blocks + b)
            for t in range(steps)
            for b in range(blocks)
        ]
        terms = terms + lax.ppermute(terms, AXES, ring)
    tip = dot(tip_inv, tip_rhs - terms)
    return solved[None], tip


def solution(mesh):
    placed = (
        P("tm", "blk", None),
        P("tm", "blk", None),
        P("tm", "blk", None),
        P("tm", None, "blk"),
        P(),
        P(),
    )
    return jax.shard_map(
        on_device,
        mesh=mesh,
        in_specs=placed,
        out_specs=(P("tm", "blk", None), P()),
        check_vma=False,
    )
```

```python
import functools

import jax
import jax.numpy as jnp
from jax import lax
from jax.experimental import pallas as pl
from jax.experimental.pallas import tpu as pltpu
from jax.sharding import PartitionSpec as P

GROUP = 8
AXES = ("tm", "blk")
HIGH = lax.Precision.HIGH
VMEM_LIMIT = 16 << 20


def dot(a, b):
    return jnp.dot(a, b, precision=HIGH, preferred_element_type=jnp.float32)


def tie(*values):
    return lax.optimization_barrier(values)


def split(value):
    upper = value.astype(jnp.bfloat16)
    lower = (value - upper.astype(jnp.float32)).astype(jnp.bfloat16)
    return upper, lower


def split_tile_kernel(piece, where, tile, upper, lower, mark, staged, arrived):
    rows, cols = tile.shape
    grid = [(e, j) for j in range(cols // piece) for e in range(rows // piece)]

    def copy(e, j):
        source_row = pl.multiple_of((where[1] ^ e) * piece, piece)
        source_col = pl.multiple_of((where[0] ^ j) * piece, piece)
        return pltpu.make_async_copy(
            tile.at[pl.ds(source_row, piece), pl.ds(source_col, piece)],
            staged.at[pl.ds(e * piece, piece), pl.ds(j * piece, piece)],
            arrived.at[e, j],
        )

    for e, j in grid:
        copy(e, j).start()
    for e, j in grid:
        copy(e, j).wait()
        at = (pl.ds(e * piece, piece), pl.ds(j * piece, piece))
        upper[at], lower[at] = split(staged[at])
    mark[...] = jnp.zeros(mark.shape, jnp.float32)


def split_tile(tile, where, piece):
    rows, cols = tile.shape
    half = jax.ShapeDtypeStruct(tile.shape, jnp.bfloat16)
    in_vmem = pl.BlockSpec(memory_space=pltpu.VMEM)
    return pl.pallas_call(
        functools.partial(split_tile_kernel, piece),
        out_shape=[half, half, jax.ShapeDtypeStruct((8, 128), jnp.float32)],
        in_specs=[pl.BlockSpec(memory_space=pltpu.SMEM), pl.BlockSpec(memory_space=pltpu.HBM)],
        out_specs=[in_vmem] * 3,
        scratch_shapes=[
            pltpu.VMEM(tile.shape, jnp.float32),
            pltpu.SemaphoreType.DMA((rows // piece, cols // piece)),
        ],
        cost_estimate=pl.CostEstimate(flops=8 * rows * cols, bytes_accessed=8 * rows * cols, transcendentals=0),
        compiler_params=pltpu.CompilerParams(vmem_limit_bytes=VMEM_LIMIT),
    )(where, pltpu.with_memory_space_constraint(tile, pltpu.HBM))


def product_kernel(count, sign, upper, lower, _, *refs):
    parts, rest = refs[:count], refs[count:]
    columns = rest[-1]
    outs = rest[:-1]
    high_count = len(outs) if sign > 0 else len(outs) // 2
    bases = outs[: len(outs) - high_count]
    outs = outs[len(outs) - high_count :]
    piece, width = parts[0].shape
    for j, part in enumerate(parts):
        at = pl.ds(j * piece, piece)
        columns[at, :width], columns[at, width:] = split(part[...])
    both = jnp.dot(upper[...], columns[...], preferred_element_type=jnp.float32)
    total = both[:, :width] + both[:, width:]
    total = total + jnp.dot(lower[...], columns[:, :width], preferred_element_type=jnp.float32)
    for e, out in enumerate(outs):
        block = total[e * piece : (e + 1) * piece]
        out[...] = block if sign > 0 else bases[e][...] - block


def tile_product(halves, parts, bases=None):
    rows, cols = halves[0].shape
    piece, width = parts[0].shape
    high_count = rows // piece
    block = jax.ShapeDtypeStruct((piece, width), jnp.float32)
    in_vmem = pl.BlockSpec(memory_space=pltpu.VMEM)
    operands = [*halves, *parts, *(bases or [])]
    return pl.pallas_call(
        functools.partial(product_kernel, len(parts), 1 if bases is None else -1),
        out_shape=[block] * high_count,
        in_specs=[in_vmem] * len(operands),
        out_specs=[in_vmem] * high_count,
        scratch_shapes=[pltpu.VMEM((cols, 2 * width), jnp.bfloat16)],
        cost_estimate=pl.CostEstimate(
            flops=6 * rows * cols * width, bytes_accessed=4 * rows * cols, transcendentals=0
        ),
        compiler_params=pltpu.CompilerParams(vmem_limit_bytes=VMEM_LIMIT),
    )(*operands)


def rows_kernel(count, *refs):
    rows, (upper, lower), outs = refs[:count], refs[count : count + 2], refs[count + 2 :]
    piece = rows[0].shape[1]
    for j, out in enumerate(outs):
        total = jnp.zeros(out.shape, jnp.float32)
        for e in range(count):
            row_upper, row_lower = split(rows[e][...])
            at = (pl.ds(e * piece, piece), pl.ds(j * piece, piece))
            total += jnp.dot(row_upper, upper[at], preferred_element_type=jnp.float32)
            total += jnp.dot(row_lower, upper[at], preferred_element_type=jnp.float32)
            total += jnp.dot(row_upper, lower[at], preferred_element_type=jnp.float32)
        out[...] = total


def rows_product(rows, halves):
    count, piece = rows[0].shape
    cols = halves[0].shape[1]
    in_vmem = pl.BlockSpec(memory_space=pltpu.VMEM)
    return pl.pallas_call(
        functools.partial(rows_kernel, len(rows)),
        out_shape=[jax.ShapeDtypeStruct((count, piece), jnp.float32)] * (cols // piece),
        in_specs=[in_vmem] * (len(rows) + 2),
        out_specs=[in_vmem] * (cols // piece),
        cost_estimate=pl.CostEstimate(
            flops=6 * count * len(rows) * piece * cols,
            bytes_accessed=4 * len(rows) * piece * cols,
            transcendentals=0,
        ),
        compiler_params=pltpu.CompilerParams(vmem_limit_bytes=VMEM_LIMIT),
    )(*rows, *halves)


def on_device(propagator, inv_diag, rhs, arrow, tip_inv, tip_rhs):
    steps = lax.axis_size("tm")
    blocks = lax.axis_size("blk")
    high_count = blocks // GROUP
    step = lax.axis_index("tm")
    position = lax.axis_index("blk")
    low = position % GROUP
    high = position // GROUP
    piece = rhs.shape[1]
    width = rhs.shape[2]

    def move(value, flip, ahead=0):
        route = [
            (t * blocks + b, (t + ahead) % steps * blocks + (b ^ flip))
            for t in range(steps)
            for b in range(blocks)
        ]
        return lax.ppermute(value, AXES, route)

    def scatter(own):
        return [move(own, flip) for flip in range(2, GROUP, 2)]

    def swap(own, sent):
        parts = []
        for part in [own, *sent]:
            parts += [part, move(part, 1)]
        return parts

    by_kernel = piece % 256 == 0 and width % 128 == 0
    where = jnp.stack([low, high]).astype(jnp.int32)

    def prepared(tile):
        return list(split_tile(tile, where, piece)) if by_kernel else [tile, tile[:8, :piece]]

    def in_order(tile):
        rows = [
            lax.dynamic_slice_in_dim(tile, (high ^ e) * piece, piece, 0) for e in range(high_count)
        ]
        tile = jnp.concatenate(rows, axis=0)
        cols = [lax.dynamic_slice_in_dim(tile, (low ^ j) * piece, piece, 1) for j in range(GROUP)]
        return jnp.concatenate(cols, axis=1)

    def apply_tile(tile, parts, bases=None):
        if by_kernel:
            return tile_product(tile, parts, bases)
        total = dot(in_order(tile[0]), jnp.concatenate(parts, axis=0))
        found = [total[e * piece : (e + 1) * piece] for e in range(high_count)]
        return found if bases is None else [b - f for b, f in zip(bases, found)]

    def row_product(rows, tile):
        if by_kernel:
            return rows_product(rows, tile[:2])
        total = dot(jnp.concatenate(rows, axis=1), in_order(tile[0]))
        return [total[:, j * piece : (j + 1) * piece] for j in range(GROUP)]

    def own_columns(found):
        odd = jnp.concatenate(found[1::2], axis=0)
        odd = move(odd, 1)
        count = found[0].shape[0]
        even = [found[j] + odd[j // 2 * count : (j // 2 + 1) * count] for j in range(0, GROUP, 2)]
        return even[0] + sum(move(even[k], 2 * k) for k in range(1, GROUP // 2))

    sent = scatter(rhs[0])
    arrows = [arrow[0]] + [move(arrow[0], e * GROUP) for e in range(1, high_count)]
    apply_g = prepared(inv_diag[0])
    sent[0], apply_g[-1], *arrows[1:] = tie(sent[0], apply_g[-1], *arrows[1:])
    partial = apply_tile(apply_g, swap(rhs[0], sent))
    for t in range(steps - 1):
        arriving = [move(partial[e], e * GROUP, 1) for e in range(high_count)]
        if t == 0:
            apply_m = prepared(propagator[0])
            arriving[0], apply_m[-1] = tie(arriving[0], apply_m[-1])
        earlier = jnp.where(step == t + 1, sum(arriving), 0.0)
        partial = apply_tile(apply_m, swap(earlier, scatter(earlier)), partial)

    others = [move(partial[e], e * GROUP) for e in range(1, high_count)]
    terms = sum(dot(arrows[e], partial[e]) for e in range(high_count))
    terms = terms + move(terms, 1)
    terms = terms + sum(move(terms, flip) for flip in range(2, GROUP, 2))
    if steps == 2 and high_count == 2:
        terms = terms + move(terms, GROUP) + move(terms, 0, 1) + move(terms, GROUP, 1)
    else:
        for e in range(high_count.bit_length() - 1):
            terms = terms + move(terms, GROUP << e)
        terms = sum(move(terms, 0, ahead) for ahead in range(steps))
    solved = partial[0] + sum(others)
    tip = dot(tip_inv, tip_rhs - terms)
    return solved[None], tip


def solution(mesh):
    placed = (
        P("tm", "blk", None),
        P("tm", "blk", None),
        P("tm", "blk", None),
        P("tm", None, "blk"),
        P(),
        P(),
    )
    return jax.shard_map(
        on_device,
        mesh=mesh,
        in_specs=placed,
        out_specs=(P("tm", "blk", None), P()),
        check_vma=False,
    )
```

```python
import functools

import jax
import jax.numpy as jnp
from jax import lax
from jax.experimental import pallas as pl
from jax.experimental.pallas import tpu as pltpu
from jax.sharding import PartitionSpec as P

GROUP = 8
AXES = ("tm", "blk")
HIGH = lax.Precision.HIGH
VMEM_LIMIT = 16 << 20
ORDER = (7, 6, 5, 4, 3, 2, 1, 0)
CHUNK = 32
ROWS = 256


def dot(a, b):
    return jnp.dot(a, b, precision=HIGH, preferred_element_type=jnp.float32)


def tie(*values):
    return lax.optimization_barrier(values)


def split(value):
    upper = value.astype(jnp.bfloat16)
    lower = (value - upper.astype(jnp.float32)).astype(jnp.bfloat16)
    return upper, lower


def three_passes(stacked, upper, lower):
    height = stacked.shape[0] // 2
    both = jnp.dot(stacked, upper, preferred_element_type=jnp.float32)
    more = jnp.dot(stacked[:height], lower, preferred_element_type=jnp.float32)
    return both[:height] + both[height:] + more


def split_tile_kernel(piece, where, tile, *refs):
    *given, upper, lower, mark, sums, staged, arrived = refs
    high_count, group = arrived.shape
    rows, values = given[:high_count], given[high_count:]
    blocks = [(e, j) for j in range(group) for e in range(high_count)]

    def copy(e, j):
        source_row = pl.multiple_of((where[1] ^ e) * piece, piece)
        source_col = pl.multiple_of((where[0] ^ j) * piece, piece)
        return pltpu.make_async_copy(
            tile.at[pl.ds(source_row, piece), pl.ds(source_col, piece)],
            staged.at[pl.ds(e * piece, piece), pl.ds(j * piece, piece)],
            arrived.at[e, j],
        )

    for e, j in blocks:
        copy(e, j).start()
    row = lax.broadcasted_iota(jnp.int32, mark.shape, 0)
    mark[...] = jnp.where(row + 1 == where[2], 1.0, 0.0)
    stacked = [jnp.concatenate(split(row[...]), axis=0) for row in rows]
    for e, value in enumerate(values):
        total = three_passes(stacked[e], *split(value[...]))
        to = (slice(None), pl.ds(group * piece, value.shape[1]))
        sums[to] = sums[to] + total if e else total
    for e, j in blocks:
        copy(e, j).wait()
        at = (pl.ds(e * piece, piece), pl.ds(j * piece, piece))
        for r in range(0, piece, CHUNK):
            part = (pl.ds(e * piece + r, CHUNK), pl.ds(j * piece, piece))
            upper[part], lower[part] = split(staged[part])
        if rows:
            total = three_passes(stacked[e], upper[at], lower[at])
            to = (slice(None), pl.ds(j * piece, piece))
            sums[to] = sums[to] + total if e else total


def split_tile(tile, where, piece, steps, rows=(), values=()):
    high_count, group = tile.shape[0] // piece, tile.shape[1] // piece
    half = jax.ShapeDtypeStruct(tile.shape, jnp.bfloat16)
    mark = jax.ShapeDtypeStruct((-(-steps // 8) * 8, 128), jnp.float32)
    sums = mark
    if rows:
        sums = jax.ShapeDtypeStruct((rows[0].shape[0], tile.shape[1] + values[0].shape[1]), jnp.float32)
    in_vmem = pl.BlockSpec(memory_space=pltpu.VMEM)
    return pl.pallas_call(
        functools.partial(split_tile_kernel, piece),
        out_shape=[half, half, mark, sums],
        in_specs=[pl.BlockSpec(memory_space=pltpu.SMEM), pl.BlockSpec(memory_space=pltpu.HBM)]
        + [in_vmem] * (len(rows) + len(values)),
        out_specs=[in_vmem] * 4,
        scratch_shapes=[
            pltpu.VMEM(tile.shape, jnp.float32),
            pltpu.SemaphoreType.DMA((high_count, group)),
        ],
        cost_estimate=pl.CostEstimate(
            flops=8 * tile.size, bytes_accessed=8 * tile.size, transcendentals=0
        ),
        compiler_params=pltpu.CompilerParams(vmem_limit_bytes=VMEM_LIMIT),
    )(where, pltpu.with_memory_space_constraint(tile, pltpu.HBM), *rows, *values)


def product_kernel(count, sign, upper, lower, _, *refs):
    parts, rest = refs[:count], refs[count:]
    columns = rest[-1]
    outs = rest[:-1]
    high_count = len(outs) if sign > 0 else len(outs) // 2
    bases = outs[: len(outs) - high_count]
    outs = outs[len(outs) - high_count :]
    piece, width = parts[0].shape
    for j, part in zip(ORDER, parts):
        at = pl.ds(j * piece, piece)
        columns[at, :width], columns[at, width:] = split(part[...])
    for e, out in enumerate(outs):
        for r in range(0, piece, ROWS):
            at, to = pl.ds(e * piece + r, ROWS), pl.ds(r, ROWS)
            both = jnp.dot(upper[at], columns[...], preferred_element_type=jnp.float32)
            more = jnp.dot(lower[at], columns[:, :width], preferred_element_type=jnp.float32)
            total = both[:, :width] + both[:, width:] + more
            out[to] = total if sign > 0 else bases[e][to] - total


def tile_product(halves, parts, bases=None):
    rows, cols = halves[0].shape
    piece, width = parts[0].shape
    high_count = rows // piece
    block = jax.ShapeDtypeStruct((piece, width), jnp.float32)
    in_vmem = pl.BlockSpec(memory_space=pltpu.VMEM)
    operands = [*halves, *(parts[j] for j in ORDER), *(bases or [])]
    return pl.pallas_call(
        functools.partial(product_kernel, len(parts), 1 if bases is None else -1),
        out_shape=[block] * high_count,
        in_specs=[in_vmem] * len(operands),
        out_specs=[in_vmem] * high_count,
        scratch_shapes=[pltpu.VMEM((cols, 2 * width), jnp.bfloat16)],
        cost_estimate=pl.CostEstimate(
            flops=6 * rows * cols * width, bytes_accessed=4 * rows * cols, transcendentals=0
        ),
        compiler_params=pltpu.CompilerParams(vmem_limit_bytes=VMEM_LIMIT),
    )(*operands)


def terms_kernel(sums, swapped, _, *refs):
    *parts, out = refs
    piece = parts[0].shape[0]
    at = pl.ds(GROUP * piece, out.shape[1])
    total = sums[:, at] + swapped[:, at]
    for j, part in zip(ORDER, parts):
        weights = sums[:, pl.ds(j * piece, piece)] + swapped[:, pl.ds((j ^ 1) * piece, piece)]
        total = total - three_passes(jnp.concatenate(split(weights), axis=0), *split(part[...]))
    out[...] = total


def terms_product(sums, swapped, mark, parts):
    in_vmem = pl.BlockSpec(memory_space=pltpu.VMEM)
    height, cols = sums.shape
    width = parts[0].shape[1]
    return pl.pallas_call(
        terms_kernel,
        out_shape=jax.ShapeDtypeStruct((height, width), jnp.float32),
        in_specs=[in_vmem] * (len(parts) + 3),
        out_specs=in_vmem,
        cost_estimate=pl.CostEstimate(
            flops=6 * height * cols * width, bytes_accessed=8 * height * cols, transcendentals=0
        ),
        compiler_params=pltpu.CompilerParams(vmem_limit_bytes=VMEM_LIMIT),
    )(sums, swapped, mark, *(parts[j] for j in ORDER))


def on_device(propagator, inv_diag, rhs, arrow, tip_inv, tip_rhs):
    steps = lax.axis_size("tm")
    blocks = lax.axis_size("blk")
    high_count = blocks // GROUP
    step = lax.axis_index("tm")
    position = lax.axis_index("blk")
    low = position % GROUP
    high = position // GROUP
    piece = rhs.shape[1]
    width = rhs.shape[2]

    def move(value, flip, ahead=0):
        route = [
            (t * blocks + b, (t + ahead) % steps * blocks + (b ^ flip))
            for t in range(steps)
            for b in range(blocks)
        ]
        return lax.ppermute(value, AXES, route)

    def scatter(own):
        return [move(own, flip) for flip in range(2, GROUP, 2)]

    def swap(own, sent):
        parts = []
        for part in [own, *sent]:
            parts += [part, move(part, 1)]
        return parts

    by_kernel = piece % 256 == 0 and width % 128 == 0
    where = jnp.stack([low, high, step]).astype(jnp.int32)

    def prepared(tile, rows=(), values=()):
        if by_kernel:
            *halves, mark, sums = split_tile(tile, where, piece, steps, rows, values)
            return halves, mark, sums
        mark = jnp.where(jnp.arange(steps)[:, None] + 1 == step, 1.0, jnp.zeros((1, width)))
        if not rows:
            return tile, mark, None
        columns = jnp.concatenate([in_order(tile), jnp.concatenate(values, axis=0)], axis=1)
        return tile, mark, dot(jnp.concatenate(rows, axis=1), columns)

    def in_order(tile):
        rows = [
            lax.dynamic_slice_in_dim(tile, (high ^ e) * piece, piece, 0) for e in range(high_count)
        ]
        tile = jnp.concatenate(rows, axis=0)
        cols = [lax.dynamic_slice_in_dim(tile, (low ^ j) * piece, piece, 1) for j in range(GROUP)]
        return jnp.concatenate(cols, axis=1)

    def apply_tile(tile, mark, parts, bases=None):
        if by_kernel:
            return tile_product([*tile, mark], parts, bases)
        total = dot(in_order(tile), jnp.concatenate(parts, axis=0))
        found = [total[e * piece : (e + 1) * piece] for e in range(high_count)]
        return found if bases is None else [b - f for b, f in zip(bases, found)]

    def subtract_product(sums, swapped, mark, parts):
        if by_kernel:
            return terms_product(sums, swapped, mark, parts)
        total = sums[:, GROUP * piece :] + swapped[:, GROUP * piece :]
        for j, part in enumerate(parts):
            k = j ^ 1
            weights = sums[:, j * piece : (j + 1) * piece] + swapped[:, k * piece : (k + 1) * piece]
            total = total - dot(weights, part)
        return total

    def tip_rounds():
        bits = [1 << k for k in range(1, blocks.bit_length() - 1)]
        rounds = []
        if steps == 2:
            rounds.append([(bits[0], 0), (0, 1), (bits[0], 1)])
            bits = bits[1:]
        elif steps > 2:
            rounds.append([(0, ahead) for ahead in range(1, steps)])
        for k in range(0, len(bits), 2):
            a, *b = bits[k : k + 2]
            rounds.append([(a, 0)] + [(f, 0) for f in b] + [(a | f, 0) for f in b])
        return rounds

    sent = scatter(rhs[0])
    arrows = [arrow[0]] + [move(arrow[0], e * GROUP) for e in range(1, high_count)]
    tile, mark, _ = prepared(inv_diag[0])
    sent[0], mark, *arrows[1:] = tie(sent[0], mark, *arrows[1:])
    mine = mark
    partial = apply_tile(tile, mark, swap(rhs[0], sent))
    if steps == 1:
        terms = sum(dot(arrows[e], partial[e]) for e in range(high_count))
        terms = terms + move(terms, 1)
    for t in range(steps - 1):
        arriving = [move(partial[e], e * GROUP, 1) for e in reversed(range(high_count))]
        if t == steps - 2:
            tile, mark, sums = prepared(propagator[0], arrows, partial)
            arriving[0], mark = tie(arriving[0], mark)
            swapped = move(sums, 1)
        elif t == 0:
            tile, mark, _ = prepared(propagator[0])
        earlier = jnp.where(mine[t : t + 1] > 0.0, sum(arriving), 0.0)
        parts = swap(earlier, scatter(earlier))
        if t == steps - 2:
            terms = mark = subtract_product(sums, swapped, mark, parts)
        partial = apply_tile(tile, mark, parts, partial)

    others = [move(partial[e], e * GROUP) for e in range(1, high_count)]
    for k, moves in enumerate(tip_rounds()):
        around = [move(terms, flip, ahead) for flip, ahead in reversed(moves)]
        if k == 1:
            *others, around[0] = tie(*others, around[0])
        terms = terms + sum(around)
    solved = partial[0] + sum(others)
    tip = dot(tip_inv, tip_rhs - terms)
    return solved[None], tip


def solution(mesh):
    placed = (
        P("tm", "blk", None),
        P("tm", "blk", None),
        P("tm", "blk", None),
        P("tm", None, "blk"),
        P(),
        P(),
    )
    return jax.shard_map(
        on_device,
        mesh=mesh,
        in_specs=placed,
        out_specs=(P("tm", "blk", None), P()),
        check_vma=False,
    )
```

```python
import functools

import jax
import jax.numpy as jnp
from jax import lax
from jax.experimental import pallas as pl
from jax.experimental.pallas import tpu as pltpu
from jax.sharding import PartitionSpec as P

GROUP = 8
AXES = ("tm", "blk")
HIGH = lax.Precision.HIGH
VMEM_LIMIT = 16 << 20
EARLY = (0, 1, 2, 3, 4, 5, 6)
LATE = (7,)
CHUNK = 32
ROWS = 256


def dot(a, b):
    return jnp.dot(a, b, precision=HIGH, preferred_element_type=jnp.float32)


def tie(*values):
    return lax.optimization_barrier(values)


def split(value):
    upper = value.astype(jnp.bfloat16)
    lower = (value - upper.astype(jnp.float32)).astype(jnp.bfloat16)
    return upper, lower


def three_passes(stacked, upper, lower):
    height = stacked.shape[0] // 2
    both = jnp.dot(stacked, upper, preferred_element_type=jnp.float32)
    more = jnp.dot(stacked[:height], lower, preferred_element_type=jnp.float32)
    return both[:height] + both[height:] + more


def split_tile_kernel(piece, where, tile, *refs):
    *given, upper, lower, mark, sums, staged, arrived = refs
    high_count, group = arrived.shape
    rows, values = given[:high_count], given[high_count:]
    blocks = [(e, j) for j in range(group) for e in range(high_count)]

    def copy(e, j):
        source_row = pl.multiple_of((where[1] ^ e) * piece, piece)
        source_col = pl.multiple_of((where[0] ^ j) * piece, piece)
        return pltpu.make_async_copy(
            tile.at[pl.ds(source_row, piece), pl.ds(source_col, piece)],
            staged.at[pl.ds(e * piece, piece), pl.ds(j * piece, piece)],
            arrived.at[e, j],
        )

    for e, j in blocks:
        copy(e, j).start()
    row = lax.broadcasted_iota(jnp.int32, mark.shape, 0)
    mark[...] = jnp.where(row + 1 == where[2], 1.0, 0.0)
    stacked = [jnp.concatenate(split(row[...]), axis=0) for row in rows]
    for e, value in enumerate(values):
        total = three_passes(stacked[e], *split(value[...]))
        to = (slice(None), pl.ds(group * piece, value.shape[1]))
        sums[to] = sums[to] + total if e else total
    for e, j in blocks:
        copy(e, j).wait()
        at = (pl.ds(e * piece, piece), pl.ds(j * piece, piece))
        for r in range(0, piece, CHUNK):
            part = (pl.ds(e * piece + r, CHUNK), pl.ds(j * piece, piece))
            upper[part], lower[part] = split(staged[part])
        if rows:
            total = three_passes(stacked[e], upper[at], lower[at])
            to = (slice(None), pl.ds(j * piece, piece))
            sums[to] = sums[to] + total if e else total


def split_tile(tile, where, piece, steps, rows=(), values=()):
    high_count, group = tile.shape[0] // piece, tile.shape[1] // piece
    half = jax.ShapeDtypeStruct(tile.shape, jnp.bfloat16)
    mark = jax.ShapeDtypeStruct((-(-steps // 8) * 8, 128), jnp.float32)
    sums = mark
    if rows:
        sums = jax.ShapeDtypeStruct((rows[0].shape[0], tile.shape[1] + values[0].shape[1]), jnp.float32)
    in_vmem = pl.BlockSpec(memory_space=pltpu.VMEM)
    return pl.pallas_call(
        functools.partial(split_tile_kernel, piece),
        out_shape=[half, half, mark, sums],
        in_specs=[pl.BlockSpec(memory_space=pltpu.SMEM), pl.BlockSpec(memory_space=pltpu.HBM)]
        + [in_vmem] * (len(rows) + len(values)),
        out_specs=[in_vmem] * 4,
        scratch_shapes=[
            pltpu.VMEM(tile.shape, jnp.float32),
            pltpu.SemaphoreType.DMA((high_count, group)),
        ],
        cost_estimate=pl.CostEstimate(
            flops=8 * tile.size, bytes_accessed=8 * tile.size, transcendentals=0
        ),
        compiler_params=pltpu.CompilerParams(vmem_limit_bytes=VMEM_LIMIT),
    )(where, pltpu.with_memory_space_constraint(tile, pltpu.HBM), *rows, *values)


def product_kernel(members, sign, blocks, height, chained, *refs):
    upper, lower, sums, swapped, _, *refs = refs
    count = blocks + (1 if height else 0)
    columns, outs, refs = refs[-1], refs[-1 - count : -1], refs[: -1 - count]
    parts, bases = refs[: len(members)], refs[len(members) :]
    piece, width = parts[0].shape
    depth = len(members) * piece
    for k, part in enumerate(parts):
        at = pl.ds(k * piece, piece)
        columns[at, :width], columns[at, width:] = split(part[...])

    def product(upper, lower):
        both = jnp.dot(upper, columns[...], preferred_element_type=jnp.float32)
        more = jnp.dot(lower, columns[:, :width], preferred_element_type=jnp.float32)
        return sign * (both[:, :width] + both[:, width:] + more)

    first = members[0] * piece
    if height:
        weights = [
            sums[:, pl.ds(j * piece, piece)] + swapped[:, pl.ds((j ^ 1) * piece, piece)]
            for j in members
        ]
        total = product(*split(jnp.concatenate(weights, axis=1)))
        if len(bases) > blocks:
            total = total + bases[blocks][...]
        else:
            at = pl.ds(GROUP * piece, width)
            total = total + sums[:, at] + swapped[:, at]
        outs[blocks][...] = total
    for e in range(blocks):
        at = (pl.ds(e * piece, piece), pl.ds(first, depth))
        total = product(upper[at], lower[at])
        outs[e][...] = bases[e][...] + total if chained else total


def tile_product(tile, members, parts, sign=1.0, bases=(), terms=None, rows=True):
    upper, lower, mark, *sums = tile
    cols = upper.shape[1]
    piece, width = parts[0].shape
    blocks = upper.shape[0] // piece if rows else 0
    block = jax.ShapeDtypeStruct((piece, width), jnp.float32)
    height = sums[0].shape[0] if terms is not None else 0
    outs = [block] * blocks
    if height:
        outs.append(jax.ShapeDtypeStruct((height, width), jnp.float32))
    in_vmem = pl.BlockSpec(memory_space=pltpu.VMEM)
    operands = [upper, lower, *(sums if height else [mark, mark]), mark]
    operands += [parts[j] for j in members]
    operands += [*(bases if rows else ()), *(terms or ())]
    depth = len(members) * piece
    return pl.pallas_call(
        functools.partial(product_kernel, members, sign, blocks, height, bool(bases)),
        out_shape=outs,
        in_specs=[in_vmem] * len(operands),
        out_specs=[in_vmem] * len(outs),
        scratch_shapes=[pltpu.VMEM((depth, 2 * width), jnp.bfloat16)],
        cost_estimate=pl.CostEstimate(
            flops=6 * (blocks * piece + height) * depth * width,
            bytes_accessed=4 * (blocks * piece + height) * depth,
            transcendentals=0,
        ),
        compiler_params=pltpu.CompilerParams(vmem_limit_bytes=VMEM_LIMIT),
    )(*operands)


def finish_kernel(count, tip_inv, tip_rhs, *refs):
    terms, (own, *others, solved, tip, solved_found, tip_found, sent) = refs[:count], refs[count:]
    total = own[...]
    for other in others:
        total = total + other[...]
    solved_found[...] = total
    first = pltpu.make_async_copy(solved_found, solved, sent.at[0])
    first.start()
    reduced = tip_rhs[...]
    for term in terms:
        reduced = reduced - term[...]
    stacked = jnp.concatenate(split(tip_inv[...]), axis=0)
    tip_found[...] = three_passes(stacked, *split(reduced))
    second = pltpu.make_async_copy(tip_found, tip, sent.at[1])
    second.start()
    first.wait()
    second.wait()


def finish(tip_inv, tip_rhs, terms, blocks):
    in_vmem = pl.BlockSpec(memory_space=pltpu.VMEM)
    shapes = [blocks[0].shape, tip_rhs.shape]
    return pl.pallas_call(
        functools.partial(finish_kernel, len(terms)),
        out_shape=[jax.ShapeDtypeStruct(shape, jnp.float32) for shape in shapes],
        in_specs=[in_vmem] * (2 + len(terms) + len(blocks)),
        out_specs=[pl.BlockSpec(memory_space=pltpu.HBM)] * 2,
        scratch_shapes=[pltpu.VMEM(shape, jnp.float32) for shape in shapes]
        + [pltpu.SemaphoreType.DMA((2,))],
        compiler_params=pltpu.CompilerParams(vmem_limit_bytes=VMEM_LIMIT),
    )(tip_inv, tip_rhs, *terms, *blocks)


def on_device(propagator, inv_diag, rhs, arrow, tip_inv, tip_rhs):
    steps = lax.axis_size("tm")
    blocks = lax.axis_size("blk")
    high_count = blocks // GROUP
    step = lax.axis_index("tm")
    position = lax.axis_index("blk")
    low = position % GROUP
    high = position // GROUP
    piece = rhs.shape[1]
    width = rhs.shape[2]

    def move(value, flip, ahead=0):
        route = [
            (t * blocks + b, (t + ahead) % steps * blocks + (b ^ flip))
            for t in range(steps)
            for b in range(blocks)
        ]
        return lax.ppermute(value, AXES, route)

    def scatter(own):
        return [move(own, flip) for flip in range(2, GROUP, 2)]

    def swap(own, sent):
        parts = []
        for part in [own, *sent]:
            parts += [part, move(part, 1)]
        return parts

    by_kernel = piece % 256 == 0 and width % 128 == 0
    where = jnp.stack([low, high, step]).astype(jnp.int32)

    def prepared(tile, rows=(), values=()):
        if by_kernel:
            *halves, mark, sums = split_tile(tile, where, piece, steps, rows, values)
            return halves, mark, sums
        mark = jnp.where(jnp.arange(steps)[:, None] + 1 == step, 1.0, jnp.zeros((1, width)))
        if not rows:
            return tile, mark, None
        columns = jnp.concatenate([in_order(tile), jnp.concatenate(values, axis=0)], axis=1)
        return tile, mark, dot(jnp.concatenate(rows, axis=1), columns)

    def in_order(tile):
        rows = [
            lax.dynamic_slice_in_dim(tile, (high ^ e) * piece, piece, 0) for e in range(high_count)
        ]
        tile = jnp.concatenate(rows, axis=0)
        cols = [lax.dynamic_slice_in_dim(tile, (low ^ j) * piece, piece, 1) for j in range(GROUP)]
        return jnp.concatenate(cols, axis=1)

    def apply_tile(tile, mark, parts, sign=1.0, bases=(), sums=()):
        if by_kernel:
            tile = [*tile, mark, *sums]
            if not sums:
                found = tile_product(tile, EARLY, parts, sign, bases)
                return tile_product(tile, LATE, parts, sign, found)
            *found, terms = tile_product(tile, EARLY, parts, sign, bases, ())
            (terms,) = tile_product(tile, LATE, parts, sign, (), (terms,), False)
            tile[2] = terms
            return [*tile_product(tile, LATE, parts, sign, found), terms]
        columns = jnp.concatenate(parts, axis=0)
        total = sign * dot(in_order(tile), columns)
        found = [total[e * piece : (e + 1) * piece] for e in range(high_count)]
        found = [b + f for b, f in zip(bases, found)] if bases else found
        if sums:
            weights, swapped = sums
            terms = weights[:, GROUP * piece :] + swapped[:, GROUP * piece :]
            for j, part in enumerate(parts):
                k = j ^ 1
                weight = weights[:, j * piece : (j + 1) * piece]
                terms = terms + sign * dot(weight + swapped[:, k * piece : (k + 1) * piece], part)
            found.append(terms)
        return found

    def tip_rounds():
        bits = [1 << k for k in range(1, blocks.bit_length() - 1)]
        rounds = []
        if steps == 2:
            rounds.append([(bits[0], 0), (0, 1), (bits[0], 1)])
            bits = bits[1:]
        elif steps > 2:
            rounds.append([(0, ahead) for ahead in range(1, steps)])
        for k in range(0, len(bits), 2):
            a, *b = bits[k : k + 2]
            rounds.insert(0, [(a, 0)] + [(f, 0) for f in b] + [(a | f, 0) for f in b])
        return rounds

    sent = scatter(rhs[0])
    arrows = [arrow[0]] + [move(arrow[0], e * GROUP) for e in range(1, high_count)]
    tile, mark, _ = prepared(inv_diag[0])
    sent[0], *arrows[1:] = tie(sent[0], *arrows[1:])
    sent[1], mark = tie(sent[1], mark)
    mine = mark
    partial = apply_tile(tile, mark, swap(rhs[0], sent))
    if steps == 1:
        terms = sum(dot(arrows[e], partial[e]) for e in range(high_count))
        terms = terms + move(terms, 1)
    for t in range(steps - 1):
        arriving = [move(partial[e], e * GROUP, 1) for e in reversed(range(high_count))]
        if t == steps - 2:
            tile, mark, sums = prepared(propagator[0], arrows, partial)
            arriving[0], mark = tie(arriving[0], mark)
            swapped = move(sums, 1)
        elif t == 0:
            tile, mark, _ = prepared(propagator[0])
        earlier = jnp.where(mine[t : t + 1] > 0.0, sum(arriving), 0.0)
        parts = swap(earlier, scatter(earlier))
        if t < steps - 2:
            partial = apply_tile(tile, mark, parts, -1.0, partial)
        else:
            *partial, terms = apply_tile(tile, mark, parts, -1.0, partial, (sums, swapped))

    others = [move(partial[e], e * GROUP) for e in range(1, high_count)]
    terms = [terms]
    for k, moves in enumerate(tip_rounds()):
        total = sum(terms[1:], terms[0])
        around = [move(total, flip, ahead) for flip, ahead in reversed(moves)]
        if k == 1:
            *others, around[0] = tie(*others, around[0])
        terms = [total, *around]
    if by_kernel:
        solved, tip = finish(tip_inv, tip_rhs, terms, [partial[0], *others])
    else:
        solved = partial[0] + sum(others)
        tip = dot(tip_inv, tip_rhs - sum(terms))
    return solved[None], tip


def solution(mesh):
    placed = (
        P("tm", "blk", None),
        P("tm", "blk", None),
        P("tm", "blk", None),
        P("tm", None, "blk"),
        P(),
        P(),
    )
    return jax.shard_map(
        on_device,
        mesh=mesh,
        in_specs=placed,
        out_specs=(P("tm", "blk", None), P()),
        check_vma=False,
    )
```

```python
import functools

import jax
import jax.numpy as jnp
from jax import lax
from jax.experimental import pallas as pl
from jax.experimental.pallas import tpu as pltpu
from jax.sharding import PartitionSpec as P

GROUP = 8
AXES = ("tm", "blk")
HIGH = lax.Precision.HIGH
VMEM_LIMIT = 16 << 20
EARLY = (0, 1, 2, 3, 4, 5, 6)
PRE = (0, 1)
REST = (2, 3, 4, 5, 6)
PRE_TIE = 2
LATE = (7,)
CHUNK = 32
ROWS = 256


def dot(a, b):
    return jnp.dot(a, b, precision=HIGH, preferred_element_type=jnp.float32)


def tie(*values):
    return lax.optimization_barrier(values)


def split(value):
    upper = value.astype(jnp.bfloat16)
    lower = (value - upper.astype(jnp.float32)).astype(jnp.bfloat16)
    return upper, lower


def three_passes(stacked, upper, lower):
    height = stacked.shape[0] // 2
    both = jnp.dot(stacked, upper, preferred_element_type=jnp.float32)
    more = jnp.dot(stacked[:height], lower, preferred_element_type=jnp.float32)
    return both[:height] + both[height:] + more


def place():
    position = lax.axis_index("blk")
    return lax.rem(position, GROUP), lax.div(position, GROUP), lax.axis_index("tm")


def split_tile_kernel(piece, tile, *refs):
    *given, upper, lower, mark, sums, staged, arrived = refs
    where = place()
    high_count, group = arrived.shape
    rows, values = given[:high_count], given[high_count:]
    blocks = [(e, j) for j in range(group) for e in range(high_count)]

    def copy(e, j):
        source_row = pl.multiple_of((where[1] ^ e) * piece, piece)
        source_col = pl.multiple_of((where[0] ^ j) * piece, piece)
        return pltpu.make_async_copy(
            tile.at[pl.ds(source_row, piece), pl.ds(source_col, piece)],
            staged.at[pl.ds(e * piece, piece), pl.ds(j * piece, piece)],
            arrived.at[e, j],
        )

    for e, j in blocks:
        copy(e, j).start()
    row = lax.broadcasted_iota(jnp.int32, mark.shape, 0)
    mark[...] = jnp.where(row + 1 == where[2], 1.0, 0.0)
    stacked = [jnp.concatenate(split(row[...]), axis=0) for row in rows]
    for e, value in enumerate(values):
        total = three_passes(stacked[e], *split(value[...]))
        to = (slice(None), pl.ds(group * piece, value.shape[1]))
        sums[to] = sums[to] + total if e else total
    for e, j in blocks:
        copy(e, j).wait()
        at = (pl.ds(e * piece, piece), pl.ds(j * piece, piece))
        for r in range(0, piece, CHUNK):
            part = (pl.ds(e * piece + r, CHUNK), pl.ds(j * piece, piece))
            upper[part], lower[part] = split(staged[part])
        if rows:
            total = three_passes(stacked[e], upper[at], lower[at])
            to = (slice(None), pl.ds(j * piece, piece))
            sums[to] = sums[to] + total if e else total


def split_tile(tile, piece, steps, rows=(), values=()):
    high_count, group = tile.shape[0] // piece, tile.shape[1] // piece
    half = jax.ShapeDtypeStruct(tile.shape, jnp.bfloat16)
    mark = jax.ShapeDtypeStruct((-(-steps // 8) * 8, 128), jnp.float32)
    sums = mark
    if rows:
        sums = jax.ShapeDtypeStruct((rows[0].shape[0], tile.shape[1] + values[0].shape[1]), jnp.float32)
    in_vmem = pl.BlockSpec(memory_space=pltpu.VMEM)
    return pl.pallas_call(
        functools.partial(split_tile_kernel, piece),
        out_shape=[half, half, mark, sums],
        in_specs=[pl.BlockSpec(memory_space=pltpu.HBM)]
        + [in_vmem] * (len(rows) + len(values)),
        out_specs=[in_vmem] * 4,
        scratch_shapes=[
            pltpu.VMEM(tile.shape, jnp.float32),
            pltpu.SemaphoreType.DMA((high_count, group)),
        ],
        cost_estimate=pl.CostEstimate(
            flops=8 * tile.size, bytes_accessed=8 * tile.size, transcendentals=0
        ),
        compiler_params=pltpu.CompilerParams(vmem_limit_bytes=VMEM_LIMIT),
    )(pltpu.with_memory_space_constraint(tile, pltpu.HBM), *rows, *values)


def product_kernel(members, sign, blocks, height, chained, *refs):
    upper, lower, sums, swapped, _, *refs = refs
    count = blocks + (1 if height else 0)
    columns, outs, refs = refs[-1], refs[-1 - count : -1], refs[: -1 - count]
    parts, bases = refs[: len(members)], refs[len(members) :]
    piece, width = parts[0].shape
    depth = len(members) * piece
    for k, part in enumerate(parts):
        at = pl.ds(k * piece, piece)
        columns[at, :width], columns[at, width:] = split(part[...])

    def product(upper, lower):
        both = jnp.dot(upper, columns[...], preferred_element_type=jnp.float32)
        more = jnp.dot(lower, columns[:, :width], preferred_element_type=jnp.float32)
        return sign * (both[:, :width] + both[:, width:] + more)

    first = members[0] * piece
    if height:
        weights = [
            sums[:, pl.ds(j * piece, piece)] + swapped[:, pl.ds((j ^ 1) * piece, piece)]
            for j in members
        ]
        total = product(*split(jnp.concatenate(weights, axis=1)))
        if len(bases) > blocks:
            total = total + bases[blocks][...]
        else:
            at = pl.ds(GROUP * piece, width)
            total = total + sums[:, at] + swapped[:, at]
        outs[blocks][...] = total
    for e in range(blocks):
        at = (pl.ds(e * piece, piece), pl.ds(first, depth))
        total = product(upper[at], lower[at])
        outs[e][...] = bases[e][...] + total if chained else total


def tile_product(tile, members, parts, sign=1.0, bases=(), terms=None, rows=True):
    upper, lower, mark, *sums = tile
    cols = upper.shape[1]
    piece, width = parts[0].shape
    blocks = upper.shape[0] // piece if rows else 0
    block = jax.ShapeDtypeStruct((piece, width), jnp.float32)
    height = sums[0].shape[0] if terms is not None else 0
    outs = [block] * blocks
    if height:
        outs.append(jax.ShapeDtypeStruct((height, width), jnp.float32))
    in_vmem = pl.BlockSpec(memory_space=pltpu.VMEM)
    operands = [upper, lower, *(sums if height else [mark, mark]), mark]
    operands += [parts[j] for j in members]
    operands += [*(bases if rows else ()), *(terms or ())]
    depth = len(members) * piece
    return pl.pallas_call(
        functools.partial(product_kernel, members, sign, blocks, height, bool(bases)),
        out_shape=outs,
        in_specs=[in_vmem] * len(operands),
        out_specs=[in_vmem] * len(outs),
        scratch_shapes=[pltpu.VMEM((depth, 2 * width), jnp.bfloat16)],
        cost_estimate=pl.CostEstimate(
            flops=6 * (blocks * piece + height) * depth * width,
            bytes_accessed=4 * (blocks * piece + height) * depth,
            transcendentals=0,
        ),
        compiler_params=pltpu.CompilerParams(vmem_limit_bytes=VMEM_LIMIT),
    )(*operands)


def finish_kernel(count, tip_inv, tip_rhs, *refs):
    terms, (own, *others, solved, tip, solved_found, tip_found, sent) = refs[:count], refs[count:]
    total = own[...]
    for other in others:
        total = total + other[...]
    solved_found[...] = total
    first = pltpu.make_async_copy(solved_found, solved, sent.at[0])
    first.start()
    reduced = tip_rhs[...]
    for term in terms:
        reduced = reduced - term[...]
    stacked = jnp.concatenate(split(tip_inv[...]), axis=0)
    tip_found[...] = three_passes(stacked, *split(reduced))
    second = pltpu.make_async_copy(tip_found, tip, sent.at[1])
    second.start()
    first.wait()
    second.wait()


def finish(tip_inv, tip_rhs, terms, blocks):
    in_vmem = pl.BlockSpec(memory_space=pltpu.VMEM)
    shapes = [blocks[0].shape, tip_rhs.shape]
    return pl.pallas_call(
        functools.partial(finish_kernel, len(terms)),
        out_shape=[jax.ShapeDtypeStruct(shape, jnp.float32) for shape in shapes],
        in_specs=[in_vmem] * (2 + len(terms) + len(blocks)),
        out_specs=[pl.BlockSpec(memory_space=pltpu.HBM)] * 2,
        scratch_shapes=[pltpu.VMEM(shape, jnp.float32) for shape in shapes]
        + [pltpu.SemaphoreType.DMA((2,))],
        compiler_params=pltpu.CompilerParams(vmem_limit_bytes=VMEM_LIMIT),
    )(tip_inv, tip_rhs, *terms, *blocks)


def on_device(propagator, inv_diag, rhs, arrow, tip_inv, tip_rhs):
    steps = lax.axis_size("tm")
    blocks = lax.axis_size("blk")
    high_count = blocks // GROUP
    step = lax.axis_index("tm")
    position = lax.axis_index("blk")
    low = position % GROUP
    high = position // GROUP
    piece = rhs.shape[1]
    width = rhs.shape[2]

    def move(value, flip, ahead=0):
        route = [
            (t * blocks + b, (t + ahead) % steps * blocks + (b ^ flip))
            for t in range(steps)
            for b in range(blocks)
        ]
        return lax.ppermute(value, AXES, route)

    def scatter(own):
        return [move(own, flip) for flip in range(2, GROUP, 2)]

    def swap(own, sent):
        parts = []
        for part in [own, *sent]:
            parts += [part, move(part, 1)]
        return parts

    by_kernel = piece % 256 == 0 and width % 128 == 0

    def prepared(tile, rows=(), values=()):
        if by_kernel:
            *halves, mark, sums = split_tile(tile, piece, steps, rows, values)
            return halves, mark, sums
        mark = jnp.where(jnp.arange(steps)[:, None] + 1 == step, 1.0, jnp.zeros((1, width)))
        if not rows:
            return tile, mark, None
        columns = jnp.concatenate([in_order(tile), jnp.concatenate(values, axis=0)], axis=1)
        return tile, mark, dot(jnp.concatenate(rows, axis=1), columns)

    def in_order(tile):
        rows = [
            lax.dynamic_slice_in_dim(tile, (high ^ e) * piece, piece, 0) for e in range(high_count)
        ]
        tile = jnp.concatenate(rows, axis=0)
        cols = [lax.dynamic_slice_in_dim(tile, (low ^ j) * piece, piece, 1) for j in range(GROUP)]
        return jnp.concatenate(cols, axis=1)

    def apply_tile(tile, mark, parts, sign=1.0, bases=(), sums=(), sums_terms=()):
        if by_kernel:
            tile = [*tile, mark, *sums]
            if not sums:
                found = tile_product(tile, EARLY, parts, sign, bases)
                return tile_product(tile, LATE, parts, sign, found)
            *found, terms = tile_product(tile, REST if sums_terms else EARLY, parts, sign, bases, sums_terms)
            (terms,) = tile_product(tile, LATE, parts, sign, (), (terms,), False)
            tile[2] = terms
            return [*tile_product(tile, LATE, parts, sign, found), terms]
        columns = jnp.concatenate(parts, axis=0)
        total = sign * dot(in_order(tile), columns)
        found = [total[e * piece : (e + 1) * piece] for e in range(high_count)]
        found = [b + f for b, f in zip(bases, found)] if bases else found
        if sums:
            weights, swapped = sums
            terms = weights[:, GROUP * piece :] + swapped[:, GROUP * piece :]
            for j, part in enumerate(parts):
                k = j ^ 1
                weight = weights[:, j * piece : (j + 1) * piece]
                terms = terms + sign * dot(weight + swapped[:, k * piece : (k + 1) * piece], part)
            found.append(terms)
        return found

    def tip_rounds():
        bits = [1 << k for k in range(1, blocks.bit_length() - 1)]
        rounds = []
        if steps == 2:
            rounds.append([(bits[0], 0), (0, 1), (bits[0], 1)])
            bits = bits[1:]
        elif steps > 2:
            rounds.append([(0, ahead) for ahead in range(1, steps)])
        for k in range(0, len(bits), 2):
            a, *b = bits[k : k + 2]
            rounds.insert(0, [(a, 0)] + [(f, 0) for f in b] + [(a | f, 0) for f in b])
        return rounds

    sent = scatter(rhs[0])
    arrows = [arrow[0]] + [move(arrow[0], e * GROUP) for e in range(1, high_count)]
    tile, mark, _ = prepared(inv_diag[0])
    sent[0], *arrows[1:] = tie(sent[0], *arrows[1:])
    sent[1], mark = tie(sent[1], mark)
    mine = mark
    partial = apply_tile(tile, mark, swap(rhs[0], sent))
    if steps == 1:
        terms = sum(dot(arrows[e], partial[e]) for e in range(high_count))
        terms = terms + move(terms, 1)
    for t in range(steps - 1):
        arriving = [move(partial[e], e * GROUP, 1) for e in reversed(range(high_count))]
        if t == steps - 2:
            tile, mark, sums = prepared(propagator[0], arrows, partial)
            arriving[0], mark = tie(arriving[0], mark)
            swapped = move(sums, 1)
        elif t == 0:
            tile, mark, _ = prepared(propagator[0])
        earlier = jnp.where(mine[t : t + 1] > 0.0, sum(arriving), 0.0)
        sent = scatter(earlier)
        parts = swap(earlier, sent)
        if t < steps - 2:
            partial = apply_tile(tile, mark, parts, -1.0, partial)
        else:
            pre = ()
            if PRE and by_kernel:
                *partial, pre = tile_product([*tile, mark, sums, swapped], PRE, parts, -1.0, partial, ())
                tied = tie(sent[PRE_TIE], pre)
                parts[2 * PRE_TIE + 2], pre = tied
                parts[2 * PRE_TIE + 3] = move(parts[2 * PRE_TIE + 2], 1)
                pre = (pre,)
            *partial, terms = apply_tile(tile, mark, parts, -1.0, partial, (sums, swapped), pre)

    others = [move(partial[e], e * GROUP) for e in range(1, high_count)]
    terms = [terms]
    for k, moves in enumerate(tip_rounds()):
        total = sum(terms[1:], terms[0])
        around = [move(total, flip, ahead) for flip, ahead in reversed(moves)]
        if k == 1:
            around[0], *others = tie(around[0], *others)
        terms = [total, *around]
    if by_kernel:
        solved, tip = finish(tip_inv, tip_rhs, terms, [partial[0], *others])
    else:
        solved = partial[0] + sum(others)
        tip = dot(tip_inv, tip_rhs - sum(terms))
    return solved[None], tip


def solution(mesh):
    placed = (
        P("tm", "blk", None),
        P("tm", "blk", None),
        P("tm", "blk", None),
        P("tm", None, "blk"),
        P(),
        P(),
    )
    return jax.shard_map(
        on_device,
        mesh=mesh,
        in_specs=placed,
        out_specs=(P("tm", "blk", None), P()),
        check_vma=False,
    )
```

```python
import functools

import jax
import jax.numpy as jnp
from jax import lax
from jax.experimental import pallas as pl
from jax.experimental.pallas import tpu as pltpu
from jax.sharding import PartitionSpec as P

GROUP = 8
AXES = ("tm", "blk")
HIGH = lax.Precision.HIGH
VMEM_LIMIT = 16 << 20
EARLY = (0, 1, 2, 3, 4, 5, 6)
PRE = (0, 1)
REST = (2, 3, 4, 5, 6)
PRE_TIE = 2
LATE = (7,)
CHUNK = 32
ROWS = 256


def dot(a, b):
    return jnp.dot(a, b, precision=HIGH, preferred_element_type=jnp.float32)


def tie(*values):
    return lax.optimization_barrier(values)


def split(value):
    upper = value.astype(jnp.bfloat16)
    lower = (value - upper.astype(jnp.float32)).astype(jnp.bfloat16)
    return upper, lower


def three_passes(stacked, upper, lower):
    height = stacked.shape[0] // 2
    both = jnp.dot(stacked, upper, preferred_element_type=jnp.float32)
    more = jnp.dot(stacked[:height], lower, preferred_element_type=jnp.float32)
    return both[:height] + both[height:] + more


def place():
    position = lax.axis_index("blk")
    return lax.rem(position, GROUP), lax.div(position, GROUP), lax.axis_index("tm")


def split_tile_kernel(piece, tile, *refs):
    *given, upper, lower, mark, sums, staged, arrived = refs
    where = place()
    high_count, group = arrived.shape
    rows, values = given[:high_count], given[high_count:]
    blocks = [(e, j) for j in range(group) for e in range(high_count)]

    def copy(e, j):
        source_row = pl.multiple_of((where[1] ^ e) * piece, piece)
        source_col = pl.multiple_of((where[0] ^ j) * piece, piece)
        return pltpu.make_async_copy(
            tile.at[pl.ds(source_row, piece), pl.ds(source_col, piece)],
            staged.at[pl.ds(e * piece, piece), pl.ds(j * piece, piece)],
            arrived.at[e, j],
        )

    for e, j in blocks:
        copy(e, j).start()
    row = lax.broadcasted_iota(jnp.int32, mark.shape, 0)
    mark[...] = jnp.where(row + 1 == where[2], 1.0, 0.0)
    stacked = [jnp.concatenate(split(row[...]), axis=0) for row in rows]
    for e, value in enumerate(values):
        total = three_passes(stacked[e], *split(value[...]))
        to = (slice(None), pl.ds(group * piece, value.shape[1]))
        sums[to] = sums[to] + total if e else total
    for e, j in blocks:
        copy(e, j).wait()
        at = (pl.ds(e * piece, piece), pl.ds(j * piece, piece))
        for r in range(0, piece, CHUNK):
            part = (pl.ds(e * piece + r, CHUNK), pl.ds(j * piece, piece))
            upper[part], lower[part] = split(staged[part])
        if rows:
            total = three_passes(stacked[e], upper[at], lower[at])
            to = (slice(None), pl.ds(j * piece, piece))
            sums[to] = sums[to] + total if e else total


def split_tile(tile, piece, steps, rows=(), values=()):
    high_count, group = tile.shape[0] // piece, tile.shape[1] // piece
    half = jax.ShapeDtypeStruct(tile.shape, jnp.bfloat16)
    mark = jax.ShapeDtypeStruct((-(-steps // 8) * 8, 128), jnp.float32)
    sums = mark
    if rows:
        sums = jax.ShapeDtypeStruct((rows[0].shape[0], tile.shape[1] + values[0].shape[1]), jnp.float32)
    in_vmem = pl.BlockSpec(memory_space=pltpu.VMEM)
    return pl.pallas_call(
        functools.partial(split_tile_kernel, piece),
        out_shape=[half, half, mark, sums],
        in_specs=[pl.BlockSpec(memory_space=pltpu.HBM)]
        + [in_vmem] * (len(rows) + len(values)),
        out_specs=[in_vmem] * 4,
        scratch_shapes=[
            pltpu.VMEM(tile.shape, jnp.float32),
            pltpu.SemaphoreType.DMA((high_count, group)),
        ],
        cost_estimate=pl.CostEstimate(
            flops=100 * tile.size, bytes_accessed=16 * tile.size, transcendentals=0
        ),
        compiler_params=pltpu.CompilerParams(vmem_limit_bytes=VMEM_LIMIT),
    )(pltpu.with_memory_space_constraint(tile, pltpu.HBM), *rows, *values)


def product_kernel(members, sign, blocks, height, chained, *refs):
    upper, lower, sums, swapped, _, *refs = refs
    count = blocks + (1 if height else 0)
    columns, outs, refs = refs[-1], refs[-1 - count : -1], refs[: -1 - count]
    parts, bases = refs[: len(members)], refs[len(members) :]
    piece, width = parts[0].shape
    depth = len(members) * piece
    for k, part in enumerate(parts):
        at = pl.ds(k * piece, piece)
        columns[at, :width], columns[at, width:] = split(part[...])

    def product(upper, lower):
        both = jnp.dot(upper, columns[...], preferred_element_type=jnp.float32)
        more = jnp.dot(lower, columns[:, :width], preferred_element_type=jnp.float32)
        return sign * (both[:, :width] + both[:, width:] + more)

    first = members[0] * piece
    if height:
        weights = [
            sums[:, pl.ds(j * piece, piece)] + swapped[:, pl.ds((j ^ 1) * piece, piece)]
            for j in members
        ]
        total = product(*split(jnp.concatenate(weights, axis=1)))
        if len(bases) > blocks:
            total = total + bases[blocks][...]
        else:
            at = pl.ds(GROUP * piece, width)
            total = total + sums[:, at] + swapped[:, at]
        outs[blocks][...] = total
    for e in range(blocks):
        at = (pl.ds(e * piece, piece), pl.ds(first, depth))
        total = product(upper[at], lower[at])
        outs[e][...] = bases[e][...] + total if chained else total


def tile_product(tile, members, parts, sign=1.0, bases=(), terms=None, rows=True):
    upper, lower, mark, *sums = tile
    cols = upper.shape[1]
    piece, width = parts[0].shape
    blocks = upper.shape[0] // piece if rows else 0
    block = jax.ShapeDtypeStruct((piece, width), jnp.float32)
    height = sums[0].shape[0] if terms is not None else 0
    outs = [block] * blocks
    if height:
        outs.append(jax.ShapeDtypeStruct((height, width), jnp.float32))
    in_vmem = pl.BlockSpec(memory_space=pltpu.VMEM)
    operands = [upper, lower, *(sums if height else [mark, mark]), mark]
    operands += [parts[j] for j in members]
    operands += [*(bases if rows else ()), *(terms or ())]
    depth = len(members) * piece
    return pl.pallas_call(
        functools.partial(product_kernel, members, sign, blocks, height, bool(bases)),
        out_shape=outs,
        in_specs=[in_vmem] * len(operands),
        out_specs=[in_vmem] * len(outs),
        scratch_shapes=[pltpu.VMEM((depth, 2 * width), jnp.bfloat16)],
        cost_estimate=pl.CostEstimate(
            flops=40 * (blocks * piece + height) * depth * width,
            bytes_accessed=40 * (blocks * piece + height) * depth,
            transcendentals=0,
        ),
        compiler_params=pltpu.CompilerParams(vmem_limit_bytes=VMEM_LIMIT),
    )(*operands)


def finish_kernel(count, tip_inv, tip_rhs, *refs):
    terms, (own, *others, solved, tip, solved_found, tip_found, sent) = refs[:count], refs[count:]
    total = own[...]
    for other in others:
        total = total + other[...]
    solved_found[...] = total
    first = pltpu.make_async_copy(solved_found, solved, sent.at[0])
    first.start()
    reduced = tip_rhs[...]
    for term in terms:
        reduced = reduced - term[...]
    stacked = jnp.concatenate(split(tip_inv[...]), axis=0)
    tip_found[...] = three_passes(stacked, *split(reduced))
    second = pltpu.make_async_copy(tip_found, tip, sent.at[1])
    second.start()
    first.wait()
    second.wait()


def finish(tip_inv, tip_rhs, terms, blocks):
    in_vmem = pl.BlockSpec(memory_space=pltpu.VMEM)
    shapes = [blocks[0].shape, tip_rhs.shape]
    return pl.pallas_call(
        functools.partial(finish_kernel, len(terms)),
        out_shape=[jax.ShapeDtypeStruct(shape, jnp.float32) for shape in shapes],
        in_specs=[in_vmem] * (2 + len(terms) + len(blocks)),
        out_specs=[pl.BlockSpec(memory_space=pltpu.HBM)] * 2,
        scratch_shapes=[pltpu.VMEM(shape, jnp.float32) for shape in shapes]
        + [pltpu.SemaphoreType.DMA((2,))],
        compiler_params=pltpu.CompilerParams(vmem_limit_bytes=VMEM_LIMIT),
    )(tip_inv, tip_rhs, *terms, *blocks)


def on_device(propagator, inv_diag, rhs, arrow, tip_inv, tip_rhs):
    steps = lax.axis_size("tm")
    blocks = lax.axis_size("blk")
    high_count = blocks // GROUP
    step = lax.axis_index("tm")
    position = lax.axis_index("blk")
    low = position % GROUP
    high = position // GROUP
    piece = rhs.shape[1]
    width = rhs.shape[2]

    def move(value, flip, ahead=0):
        route = [
            (t * blocks + b, (t + ahead) % steps * blocks + (b ^ flip))
            for t in range(steps)
            for b in range(blocks)
        ]
        return lax.ppermute(value, AXES, route)

    def scatter(own):
        return [move(own, flip) for flip in range(2, GROUP, 2)]

    def swap(own, sent):
        parts = []
        for part in [own, *sent]:
            parts += [part, move(part, 1)]
        return parts

    by_kernel = piece % 256 == 0 and width % 128 == 0

    def prepared(tile, rows=(), values=()):
        if by_kernel:
            *halves, mark, sums = split_tile(tile, piece, steps, rows, values)
            return halves, mark, sums
        mark = jnp.where(jnp.arange(steps)[:, None] + 1 == step, 1.0, jnp.zeros((1, width)))
        if not rows:
            return tile, mark, None
        columns = jnp.concatenate([in_order(tile), jnp.concatenate(values, axis=0)], axis=1)
        return tile, mark, dot(jnp.concatenate(rows, axis=1), columns)

    def in_order(tile):
        rows = [
            lax.dynamic_slice_in_dim(tile, (high ^ e) * piece, piece, 0) for e in range(high_count)
        ]
        tile = jnp.concatenate(rows, axis=0)
        cols = [lax.dynamic_slice_in_dim(tile, (low ^ j) * piece, piece, 1) for j in range(GROUP)]
        return jnp.concatenate(cols, axis=1)

    def apply_tile(tile, mark, parts, sign=1.0, bases=(), sums=(), sums_terms=()):
        if by_kernel:
            tile = [*tile, mark, *sums]
            if not sums:
                found = tile_product(tile, EARLY, parts, sign, bases)
                return tile_product(tile, LATE, parts, sign, found)
            *found, terms = tile_product(tile, REST if sums_terms else EARLY, parts, sign, bases, sums_terms)
            (terms,) = tile_product(tile, LATE, parts, sign, (), (terms,), False)
            tile[2] = terms
            return [*tile_product(tile, LATE, parts, sign, found), terms]
        columns = jnp.concatenate(parts, axis=0)
        total = sign * dot(in_order(tile), columns)
        found = [total[e * piece : (e + 1) * piece] for e in range(high_count)]
        found = [b + f for b, f in zip(bases, found)] if bases else found
        if sums:
            weights, swapped = sums
            terms = weights[:, GROUP * piece :] + swapped[:, GROUP * piece :]
            for j, part in enumerate(parts):
                k = j ^ 1
                weight = weights[:, j * piece : (j + 1) * piece]
                terms = terms + sign * dot(weight + swapped[:, k * piece : (k + 1) * piece], part)
            found.append(terms)
        return found

    def tip_rounds():
        bits = [1 << k for k in range(1, blocks.bit_length() - 1)]
        rounds = []
        if steps == 2:
            rounds.append([(bits[0], 0), (0, 1), (bits[0], 1)])
            bits = bits[1:]
        elif steps > 2:
            rounds.append([(0, ahead) for ahead in range(1, steps)])
        for k in range(0, len(bits), 2):
            a, *b = bits[k : k + 2]
            rounds.insert(0, [(a, 0)] + [(f, 0) for f in b] + [(a | f, 0) for f in b])
        return rounds

    sent = scatter(rhs[0])
    arrows = [arrow[0]] + [move(arrow[0], e * GROUP) for e in range(1, high_count)]
    tile, mark, _ = prepared(inv_diag[0])
    *arrows[1:], mark = tie(*arrows[1:], mark)
    sent[1], mark = tie(sent[1], mark)
    mine = mark
    partial = apply_tile(tile, mark, swap(rhs[0], sent))
    if steps == 1:
        terms = sum(dot(arrows[e], partial[e]) for e in range(high_count))
        terms = terms + move(terms, 1)
    for t in range(steps - 1):
        arriving = [move(partial[e], e * GROUP, 1) for e in reversed(range(high_count))]
        if t == steps - 2:
            tile, mark, sums = prepared(propagator[0], arrows, partial)
            arriving[0], mark = tie(arriving[0], mark)
            swapped = move(sums, 1)
        elif t == 0:
            tile, mark, _ = prepared(propagator[0])
        earlier = jnp.where(mine[t : t + 1] > 0.0, sum(arriving[::-1]), 0.0)
        sent = scatter(earlier)
        parts = swap(earlier, sent)
        if t < steps - 2:
            partial = apply_tile(tile, mark, parts, -1.0, partial)
        else:
            pre = ()
            if PRE and by_kernel:
                *partial, pre = tile_product([*tile, mark, sums, swapped], PRE, parts, -1.0, partial, ())
                tied = tie(sent[PRE_TIE], pre)
                parts[2 * PRE_TIE + 2], pre = tied
                parts[2 * PRE_TIE + 3] = move(parts[2 * PRE_TIE + 2], 1)
                pre = (pre,)
            *partial, terms = apply_tile(tile, mark, parts, -1.0, partial, (sums, swapped), pre)

    others = [move(partial[e], e * GROUP) for e in range(1, high_count)]
    terms = [terms]
    for k, moves in enumerate(tip_rounds()):
        total = sum(terms[1:], terms[0])
        around = [move(total, flip, ahead) for flip, ahead in reversed(moves)]
        if k == 1:
            *others, around[0] = tie(*others, around[0])
        terms = [total, *around]
    if by_kernel:
        solved, tip = finish(tip_inv, tip_rhs, terms, [partial[0], *others])
    else:
        solved = partial[0] + sum(others)
        tip = dot(tip_inv, tip_rhs - sum(terms))
    return solved[None], tip


def solution(mesh):
    placed = (
        P("tm", "blk", None),
        P("tm", "blk", None),
        P("tm", "blk", None),
        P("tm", None, "blk"),
        P(),
        P(),
    )
    return jax.shard_map(
        on_device,
        mesh=mesh,
        in_specs=placed,
        out_specs=(P("tm", "blk", None), P()),
        check_vma=False,
    )
```
